128 devices in a mesh: rep: 16 (over z_hi, x, core), tp: 8 (over y, z_lo).
Axes of the slice: x: 4, y: 4, z: 4 (z_hi: 2, z_lo: 2; z = z_hi * 2 + z_lo), core: 2. Of those that a mesh axis runs over, the one named last changes fastest.
Arguments:
- hidden: bfloat16 [16, 4, 5120], P('rep'), may hold values from -6 to 6
- in_gain: bfloat16 [5120], replicated, may hold values from 0.099609375 to 1.8984375
- old_qkv: bfloat16 [5120, 6144], P(None, 'tp'), may hold values from -0.078125 to 0.078125
- old_out: bfloat16 [4096, 5120], P('tp'), may hold values from -0.09375 to 0.09375
- q_gain: bfloat16 [128], replicated, may hold values from 0.099609375 to 1.8984375
- k_gain: bfloat16 [128], replicated, may hold values from 2 to 3
- cache_keys: bfloat16 [16, 8192, 8, 128], P('rep', None, 'tp'), may hold values from -360 to 360
- stored_values: bfloat16 [16, 8192, 8, 128], P('rep', None, 'tp'), may hold values from -6 to 6
- cache_lengths: int32 [16], P('rep'), may hold values from 2048 to 8192, as said below
- new_qkv: bfloat16 [5120, 6144], P(('rep', 'tp')), may hold values from -0.078125 to 0.078125
Outputs:
- attended: bfloat16 [16, 4, 5120], P('rep')
- rollout_qkv: bfloat16 [5120, 6144], P(None, 'tp')
The draws below stay inside these ranges and needn't reach their ends.
Inputs may be any that keep to these rules, and one draw needn't show every extreme that they name: `cache_lengths`: some sequence has exactly 8192 filled slots in every draw.
All inputs are finite; a program needn't handle non-finite values.
Results may differ from the reference program's by a relative error of at most 0.015.
The reference program's roundings to bfloat16 on the way count: a program that leaves them out, or rounds other values in their place, can miss the bound.
Values may be sent and summed in bfloat16 or wider, within the bound.
No kernel may reach another device: no remote copies, remote signals or barrier semaphores. Data moves between devices by JAX's collectives and lax.ppermute only.
A program may use at most 128 MiB of HBM per device.

```python
import jax
import jax.numpy as jnp
from jax import lax

D = 5120
QUERY_HEADS = 32
KEY_VALUE_HEADS = 8
HEAD_DIMENSION = 128
CACHE_SLOTS = 8192
DECODE_STEPS = 4
SEQUENCE_TOTAL = 16
QKV = 6144


def draw_cache_keys(key, part):
    key = jax.random.fold_in(key, 11)
    first_leg = jax.random.fold_in(key, 0)
    random_noise = jnp.clip(jax.random.normal(first_leg, (SEQUENCE_TOTAL, CACHE_SLOTS, KEY_VALUE_HEADS, HEAD_DIMENSION), jnp.float32), -4.5, 4.5)
    scale_factors = 2.5 * jnp.ones((SEQUENCE_TOTAL, 1, KEY_VALUE_HEADS, 1), jnp.float32)
    return (random_noise * scale_factors).astype(jnp.bfloat16)


def draw_cache_lengths(key, part):
    key = jax.random.fold_in(key, 12)
    first_leg, second_leg = jax.random.split(key)
    counts = jax.random.randint(first_leg, (SEQUENCE_TOTAL,), CACHE_SLOTS // 4, CACHE_SLOTS + 1)
    chosen = jax.random.randint(second_leg, (), 0, SEQUENCE_TOTAL)
    return jnp.where(jnp.arange(SEQUENCE_TOTAL) == chosen, CACHE_SLOTS, counts).astype(jnp.int32)


def levels(key, dims, cuts, least, largest):
    level = 1.0
    for dim, parts in cuts:
        steps = jax.random.uniform(jax.random.fold_in(jax.random.fold_in(key, 6), dim), (parts,), jnp.float32, least / len(cuts), largest / len(cuts))
        level = level * jnp.repeat(jnp.exp(steps), dims[dim] // parts).reshape((-1,) + (1,) * (len(dims) - 1 - dim))
    return level


def bell_draw(own_key, shape, spread, reach, pieces=(), dtype=jnp.bfloat16):
    array = spread * jax.random.normal(own_key, shape, jnp.float32)
    if pieces:
        array = array * levels(own_key, shape, pieces, -0.22, 0.18)
    return jnp.clip(array, -reach, reach).astype(dtype)


def setup_inputs(seed: int = 0) -> dict:
    keys = jax.random.split(jax.random.key(seed), 11)
    hidden = bell_draw(keys[0], (SEQUENCE_TOTAL, DECODE_STEPS, D), 1.0, 6.0, ((0, 16),))
    in_gain = jnp.clip(1.0 + 0.18 * jax.random.normal(keys[1], (D,), jnp.float32), 0.099609375, 1.8984375).astype(jnp.bfloat16)
    old_qkv = bell_draw(keys[2], (D, QKV), D ** -0.5, 0.078125, ((1, 8),))
    old_out = bell_draw(keys[3], (QUERY_HEADS * HEAD_DIMENSION, D), (QUERY_HEADS * HEAD_DIMENSION) ** -0.5, 0.09375, ((0, 8),))
    q_gain = jnp.clip(1.0 + 0.18 * jax.random.normal(keys[4], (HEAD_DIMENSION,), jnp.float32), 0.099609375, 1.8984375).astype(jnp.bfloat16)
    k_gain = jnp.clip(jax.random.uniform(keys[5], (HEAD_DIMENSION,), jnp.float32, 2.0, 3.0), 2.0, 3.0).astype(jnp.bfloat16)
    cache_keys = draw_cache_keys(jax.random.fold_in(keys[10], 71), 0)
    stored_values = bell_draw(keys[7], (SEQUENCE_TOTAL, CACHE_SLOTS, KEY_VALUE_HEADS, HEAD_DIMENSION), 1.0, 6.0, ((0, 16), (2, 8)))
    cache_lengths = draw_cache_lengths(jax.random.fold_in(keys[10], 71), 0)
    new_qkv = bell_draw(keys[9], (D, QKV), D ** -0.5, 0.078125, ((0, 128),))
    return {"hidden": hidden, "in_gain": in_gain, "old_qkv": old_qkv, "old_out": old_out, "q_gain": q_gain, "k_gain": k_gain, "cache_keys": cache_keys, "stored_values": stored_values, "cache_lengths": cache_lengths, "new_qkv": new_qkv}


def rms_norm(values, gain):
    mean_sq = lax.optimization_barrier(jnp.mean(values * values, axis=-1, keepdims=True))
    return values * lax.rsqrt(mean_sq + 1e-06) * gain

def rotate_pairs(values, positions):
    half_dim = HEAD_DIMENSION // 2
    frequency = 1000000.0 ** (-(jnp.arange(half_dim).astype(jnp.float32) * 2.0 / HEAD_DIMENSION))
    angles = positions[..., None] * frequency
    cosine = jnp.cos(angles)
    sine_part = jnp.sin(angles)
    first_leg = values[..., :half_dim]
    second_leg = values[..., half_dim:]
    return jnp.concatenate([first_leg * cosine - second_leg * sine_part, second_leg * cosine + first_leg * sine_part], axis=-1)

def attend_one(queries, keys_new, values_new, keys_old, values_old, length):
    scale = 1.0 / jnp.sqrt(jnp.float32(HEAD_DIMENSION))
    score_old = jnp.einsum('thgd,phd->thgp', queries.astype(jnp.float32), keys_old.astype(jnp.float32)) * scale
    score_new = jnp.einsum('thgd,uhd->thgu', queries.astype(jnp.float32), keys_new.astype(jnp.float32)) * scale
    slot_ok = jnp.arange(CACHE_SLOTS).astype(jnp.int32) < length
    step_ok = jnp.arange(DECODE_STEPS)[None, :] <= jnp.arange(DECODE_STEPS)[:, None]
    score_old = jnp.where(slot_ok[None, None, None, :], score_old, -1e+30)
    score_new = jnp.where(step_ok[:, None, None, :], score_new, -1e+30)
    top_score = jnp.maximum(lax.optimization_barrier(jnp.max(score_old, axis=-1, keepdims=True)), lax.optimization_barrier(jnp.max(score_new, axis=-1, keepdims=True)))
    exp_old = jnp.where(slot_ok[None, None, None, :], jnp.exp(score_old - top_score), 0.0)
    exp_new = jnp.where(step_ok[:, None, None, :], jnp.exp(score_new - top_score), 0.0)
    total = lax.optimization_barrier(jnp.sum(exp_old, axis=-1, keepdims=True)) + lax.optimization_barrier(jnp.sum(exp_new, axis=-1, keepdims=True))
    weight_old = (exp_old / total).astype(jnp.bfloat16)
    weight_new = (exp_new / total).astype(jnp.bfloat16)
    mixed = jnp.einsum('thgp,phd->thgd', weight_old.astype(jnp.float32), values_old.astype(jnp.float32))
    mixed = mixed + jnp.einsum('thgu,uhd->thgd', weight_new.astype(jnp.float32), values_new.astype(jnp.float32))
    return mixed.astype(jnp.bfloat16).reshape(DECODE_STEPS, QUERY_HEADS * HEAD_DIMENSION)

def reference(hidden, in_gain, old_qkv, old_out, q_gain, k_gain, cache_keys, stored_values, cache_lengths, new_qkv):
    query_group = QUERY_HEADS // KEY_VALUE_HEADS
    normed = rms_norm(hidden.astype(jnp.float32), in_gain.astype(jnp.float32)).astype(jnp.bfloat16)
    projected_rows = jnp.dot(normed.reshape(SEQUENCE_TOTAL * DECODE_STEPS, D), old_qkv, preferred_element_type=jnp.float32)
    projected_rows = projected_rows.reshape(SEQUENCE_TOTAL, DECODE_STEPS, KEY_VALUE_HEADS, query_group + 2, HEAD_DIMENSION)
    positions = (cache_lengths.astype(jnp.int32)[:, None] + jnp.arange(DECODE_STEPS).astype(jnp.int32)[None, :]).astype(jnp.float32)
    queries = rotate_pairs(rms_norm(projected_rows[:, :, :, :query_group, :], q_gain.astype(jnp.float32)), positions[:, :, None, None]).astype(jnp.bfloat16)
    keys_new = rotate_pairs(rms_norm(projected_rows[:, :, :, query_group, :], k_gain.astype(jnp.float32)), positions[:, :, None]).astype(jnp.bfloat16)
    values_new = projected_rows[:, :, :, query_group + 1, :].astype(jnp.bfloat16)

    def one_sequence(items):
        return attend_one(*items)
    heads = lax.map(one_sequence, (queries, keys_new, values_new, cache_keys, stored_values, cache_lengths.astype(jnp.int32)))
    attended = jnp.dot(heads.reshape(SEQUENCE_TOTAL * DECODE_STEPS, QUERY_HEADS * HEAD_DIMENSION), old_out, preferred_element_type=jnp.float32)
    attended = attended.reshape(SEQUENCE_TOTAL, DECODE_STEPS, D).astype(jnp.bfloat16)
    return (attended, new_qkv)
```

```python
import jax
import jax.numpy as jnp
from jax import lax
from jax.experimental import pallas as pl
from jax.experimental.pallas import tpu as pltpu
from jax.sharding import PartitionSpec as P

BF16 = jnp.bfloat16
F32 = jnp.float32
STEPS = 4
GROUP = 4
HEAD = 128
ROWS = STEPS * GROUP


def rope_tables(cache_lengths):
    half = HEAD // 2
    frequency = 1000000.0 ** (-(jnp.arange(half).astype(F32) * 2.0 / HEAD))
    positions = (cache_lengths[:, None] + jnp.arange(STEPS)[None, :]).astype(F32)
    angles = positions[0, :, None] * frequency
    cosine = jnp.cos(angles)
    sine = jnp.sin(angles)
    return jnp.concatenate([cosine, cosine], axis=-1), jnp.concatenate([-sine, sine], axis=-1)


def attention_kernel(
    length_ref, hidden_ref, in_gain_ref, q_gain_ref, k_gain_ref, cos_ref, sin_ref,
    qkv_hbm, keys_hbm, values_hbm, out_hbm,
    partial_ref,
    qkv, keys, values, wout, scores, sems,
):
    width = qkv.shape[0]
    slots = keys.shape[0]
    qkv_parts, key_parts, value_parts, out_parts = 5, 2, 2, 4
    copies = {}
    sem = 0
    for name, src, dst, parts in (
        ("qkv", qkv_hbm, qkv, qkv_parts),
        ("keys", keys_hbm, keys, key_parts),
        ("values", values_hbm, values, value_parts),
        ("out", out_hbm, wout, out_parts),
    ):
        rows = src.shape[0] // parts
        for part in range(parts):
            span = pl.ds(part * rows, rows)
            copies[name, part] = pltpu.make_async_copy(src.at[span], dst.at[span], sems.at[sem])
            copies[name, part].start()
            sem += 1

    states = hidden_ref[...].astype(F32)
    mean_sq = jnp.mean(states * states, axis=-1, keepdims=True)
    normed = (states * lax.rsqrt(mean_sq + 1e-06) * in_gain_ref[...].astype(F32)).astype(BF16)

    depth = width // qkv_parts
    projected = None
    for part in range(qkv_parts):
        copies["qkv", part].wait()
        term = jnp.dot(
            normed[:, part * depth : (part + 1) * depth],
            qkv[part * depth : (part + 1) * depth, :],
            preferred_element_type=F32,
        )
        projected = term if projected is None else projected + term

    cosine = cos_ref[...]
    sine = sin_ref[...]

    def norm_rotate(block, gain):
        mean = jnp.mean(block * block, axis=-1, keepdims=True)
        block = block * lax.rsqrt(mean + 1e-06) * gain
        swapped = jnp.concatenate([block[:, HEAD // 2 :], block[:, : HEAD // 2]], axis=-1)
        return block * cosine + swapped * sine

    q_gain = q_gain_ref[...].astype(F32)
    queries = jnp.concatenate(
        [norm_rotate(projected[:, j * HEAD : (j + 1) * HEAD], q_gain) for j in range(GROUP)], axis=0
    ).astype(BF16)
    blank = jnp.zeros((ROWS - STEPS, HEAD), F32)
    keys_new = jnp.concatenate(
        [norm_rotate(projected[:, GROUP * HEAD : (GROUP + 1) * HEAD], k_gain_ref[...].astype(F32)), blank],
        axis=0,
    ).astype(BF16)
    values_new = jnp.concatenate([projected[:, (GROUP + 1) * HEAD :], blank], axis=0).astype(BF16)

    length = length_ref[0]
    scale = 1.0 / jnp.sqrt(F32(HEAD))
    contract = (((1,), (1,)), ((), ()))
    new = lax.dot_general(queries, keys_new, contract, preferred_element_type=F32) * scale
    row = lax.broadcasted_iota(jnp.int32, (ROWS, ROWS), 0) % STEPS
    step_ok = lax.broadcasted_iota(jnp.int32, (ROWS, ROWS), 1) <= row
    new = jnp.where(step_ok, new, -1e30)
    top = jnp.max(new, axis=-1, keepdims=True)
    span = slots // key_parts
    for part in range(key_parts):
        copies["keys", part].wait()
        score = lax.dot_general(
            queries, keys[part * span : (part + 1) * span, :], contract, preferred_element_type=F32
        ) * scale
        slot = lax.broadcasted_iota(jnp.int32, (ROWS, span), 1) + part * span
        score = jnp.where(slot < length, score, -1e30)
        scores[:, part * span : (part + 1) * span] = score
        top = jnp.maximum(top, jnp.max(score, axis=-1, keepdims=True))
    exp_new = jnp.where(step_ok, jnp.exp(new - top), 0.0)
    total = jnp.sum(exp_new, axis=-1, keepdims=True)
    for part in range(key_parts):
        exp_old = jnp.exp(scores[:, part * span : (part + 1) * span] - top)
        scores[:, part * span : (part + 1) * span] = exp_old
        total = total + jnp.sum(exp_old, axis=-1, keepdims=True)
    weight_new = (exp_new / total).astype(BF16)
    mixed = jnp.dot(weight_new, values_new, preferred_element_type=F32)
    span = slots // value_parts
    for part in range(value_parts):
        copies["values", part].wait()
        weight = (scores[:, part * span : (part + 1) * span] / total).astype(BF16)
        mixed = mixed + jnp.dot(
            weight, values[part * span : (part + 1) * span, :], preferred_element_type=F32
        )
    heads = jnp.concatenate([mixed[j * STEPS : (j + 1) * STEPS, :] for j in range(GROUP)], axis=-1)
    heads = heads.astype(BF16)
    partial = None
    depth = wout.shape[0] // out_parts
    for part in range(out_parts):
        copies["out", part].wait()
        term = jnp.dot(
            heads[:, part * depth : (part + 1) * depth],
            wout[part * depth : (part + 1) * depth, :],
            preferred_element_type=F32,
        )
        partial = term if partial is None else partial + term
    partial_ref[...] = partial.astype(BF16)


def attention(hidden, in_gain, old_qkv, old_out, q_gain, k_gain, cache_keys, stored_values, cache_lengths):
    width = hidden.shape[-1]
    slots = cache_keys.shape[1]
    cosine, sine = rope_tables(cache_lengths)
    vmem = pl.BlockSpec(memory_space=pltpu.VMEM)
    hbm = pl.BlockSpec(memory_space=pl.ANY)
    return pl.pallas_call(
        attention_kernel,
        out_shape=jax.ShapeDtypeStruct((STEPS, width), BF16),
        in_specs=[pl.BlockSpec(memory_space=pltpu.SMEM)] + [vmem] * 6 + [hbm] * 4,
        out_specs=vmem,
        scratch_shapes=[
            pltpu.VMEM(old_qkv.shape, BF16),
            pltpu.VMEM((slots, HEAD), BF16),
            pltpu.VMEM((slots, HEAD), BF16),
            pltpu.VMEM(old_out.shape, BF16),
            pltpu.VMEM((ROWS, slots), F32),
            pltpu.SemaphoreType.DMA((13,)),
        ],
        compiler_params=pltpu.CompilerParams(vmem_limit_bytes=40 * 1024 * 1024),
        cost_estimate=pl.CostEstimate(flops=120_000_000, bytes_accessed=17_400_000, transcendentals=140_000),
        name="attention",
    )(
        cache_lengths, hidden.reshape(STEPS, width), in_gain.reshape(1, width), q_gain.reshape(1, HEAD),
        k_gain.reshape(1, HEAD), cosine, sine, old_qkv, cache_keys.reshape(slots, HEAD),
        stored_values.reshape(slots, HEAD), old_out,
    )


def place(pieces, shape, previous=None):
    slots = jnp.stack([slot for _, slot, _ in pieces]).astype(jnp.int32)
    arrays = [array for array, _, _ in pieces]
    starts = [start for _, _, start in pieces]
    count = len(arrays)

    def kernel(slots_ref, *refs):
        sources, out, sems = refs[:count], refs[-2], refs[-1]
        copies = []
        for i in range(count):
            copy = pltpu.make_async_copy(
                sources[i], out.at[slots_ref[i], pl.ds(starts[i], sources[i].shape[0])], sems.at[i]
            )
            copy.start()
            copies.append(copy)
        for copy in copies:
            copy.wait()

    hbm = pl.BlockSpec(memory_space=pl.ANY)
    operands = [slots] + arrays + ([] if previous is None else [previous])
    size = sum(a.size for a in arrays) * 2
    return pl.pallas_call(
        kernel,
        out_shape=jax.ShapeDtypeStruct(shape, BF16),
        in_specs=[pl.BlockSpec(memory_space=pltpu.SMEM)] + [hbm] * (len(operands) - 1),
        out_specs=hbm,
        scratch_shapes=[pltpu.SemaphoreType.DMA((count,))],
        input_output_aliases={} if previous is None else {len(operands) - 1: 0},
        cost_estimate=pl.CostEstimate(flops=0, bytes_accessed=2 * size, transcendentals=0),
        name="place",
    )(*operands)


def reshard(new_qkv):
    rows, columns = new_qkv.shape
    tp = lax.axis_size("tp")
    rep = lax.axis_size("rep")
    me = lax.axis_index("rep")
    z, x, core = me // 8, me // 2 % 4, me % 2

    def index(z, x, core):
        return (z * 4 + x) * 2 + core

    def send(array, dz=0, dx=0, dc=0):
        pairs = []
        for i in range(rep):
            a, b, c = i // 8, i // 2 % 4, i % 2
            pairs.append((i, index((a + dz) % 2, (b + dx) % 4, (c + dc) % 2)))
        return lax.ppermute(array, "rep", pairs)

    def slot(dz, dx, dc):
        return index((z + dz) % 2, (x + dx) % 4, (core + dc) % 2)

    half = tp // 2
    blocks = new_qkv.reshape(rows, tp, columns // tp).transpose(1, 0, 2)
    own = lax.all_to_all(blocks, "tp", split_axis=0, concat_axis=0, tiled=True)
    left = send(own, dx=1)
    right = send(own, dx=-1)
    other = send(own, dz=1)
    core_own = send(own, dc=1)
    far_a = send(left[:half], dx=1)
    far_b = send(right[half:], dx=-1)
    other_left = send(other, dx=1)
    other_right = send(other, dx=-1)
    core_first = send(jnp.concatenate([left, right, other]), dc=1)
    other_far_a = send(other_left[:half], dx=1)
    other_far_b = send(other_right[half:], dx=-1)
    core_second = send(jnp.concatenate([far_a, far_b, other_left, other_right]), dc=1)
    core_third = send(jnp.concatenate([other_far_a, other_far_b]), dc=1)

    shape = (rep, tp, rows, columns // tp)
    out = place(
        [
            (own, slot(0, 0, 0), 0),
            (core_own, slot(0, 0, 1), 0),
            (left, slot(0, -1, 0), 0),
            (right, slot(0, 1, 0), 0),
            (other, slot(1, 0, 0), 0),
        ],
        shape,
    )
    out = place(
        [
            (core_first[:tp], slot(0, -1, 1), 0),
            (core_first[tp : 2 * tp], slot(0, 1, 1), 0),
            (core_first[2 * tp :], slot(1, 0, 1), 0),
            (far_a, slot(0, 2, 0), 0),
            (far_b, slot(0, 2, 0), half),
            (other_left, slot(1, -1, 0), 0),
            (other_right, slot(1, 1, 0), 0),
        ],
        shape,
        out,
    )
    out = place(
        [
            (core_second[:tp], slot(0, 2, 1), 0),
            (core_second[tp : 2 * tp], slot(1, -1, 1), 0),
            (core_second[2 * tp :], slot(1, 1, 1), 0),
            (other_far_a, slot(1, 2, 0), 0),
            (other_far_b, slot(1, 2, 0), half),
            (core_third, slot(1, 2, 1), 0),
        ],
        shape,
        out,
    )
    return out.reshape(rep * tp * rows, columns // tp)


def body(
    hidden, in_gain, old_qkv, old_out, q_gain, k_gain, cache_keys, stored_values, cache_lengths, new_qkv
):
    rollout_qkv = reshard(new_qkv)
    partial = attention(
        hidden, in_gain, old_qkv, old_out, q_gain, k_gain, cache_keys, stored_values, cache_lengths
    )
    tp = lax.axis_size("tp")
    copies = jnp.broadcast_to(partial[None], (tp,) + partial.shape)
    terms = lax.all_to_all(copies, "tp", split_axis=0, concat_axis=0, tiled=True)
    attended = jnp.sum(terms.astype(F32), axis=0).astype(BF16)
    return attended.reshape(hidden.shape), rollout_qkv


def solution(mesh):
    in_specs = (
        P("rep", None, None),
        P(),
        P(None, "tp"),
        P("tp", None),
        P(),
        P(),
        P("rep", None, "tp", None),
        P("rep", None, "tp", None),
        P("rep"),
        P(("rep", "tp"), None),
    )
    out_specs = (P("rep", None, None), P(None, "tp"))
    return jax.shard_map(body, mesh=mesh, in_specs=in_specs, out_specs=out_specs, check_vma=False)
```

```python
import jax
import jax.numpy as jnp
from jax import lax
from jax.experimental import pallas as pl
from jax.experimental.pallas import tpu as pltpu
from jax.sharding import PartitionSpec as P

BF16 = jnp.bfloat16
F32 = jnp.float32
STEPS = 4
GROUP = 4
HEAD = 128
ROWS = STEPS * GROUP
REP = ("z_hi", "x", "core")
TP = "tp"


def rope_tables(cache_lengths):
    half = HEAD // 2
    frequency = 1000000.0 ** (-(jnp.arange(half).astype(F32) * 2.0 / HEAD))
    positions = (cache_lengths[:, None] + jnp.arange(STEPS)[None, :]).astype(F32)
    angles = positions[0, :, None] * frequency
    cosine = jnp.cos(angles)
    sine = jnp.sin(angles)
    return jnp.concatenate([cosine, cosine], axis=-1), jnp.concatenate([-sine, sine], axis=-1)


def attention_kernel(
    length_ref, cos_ref, sin_ref,
    hidden_hbm, in_gain_hbm, q_gain_hbm, k_gain_hbm, qkv_hbm, keys_hbm, values_hbm, out_hbm,
    partial_ref,
    hidden, in_gain, q_gain, k_gain, qkv, keys, values, wout, scores, sems,
):
    width = qkv.shape[0]
    slots = keys.shape[0]
    qkv_parts, key_parts, value_parts, out_parts = 5, 2, 2, 4
    copies = {}
    sem = 0
    for name, src, dst, parts in (
        ("hidden", hidden_hbm, hidden, 1),
        ("in_gain", in_gain_hbm, in_gain, 1),
        ("q_gain", q_gain_hbm, q_gain, 1),
        ("k_gain", k_gain_hbm, k_gain, 1),
        ("qkv", qkv_hbm, qkv, qkv_parts),
        ("keys", keys_hbm, keys, key_parts),
        ("values", values_hbm, values, value_parts),
        ("out", out_hbm, wout, out_parts),
    ):
        rows = src.shape[0] // parts
        for part in range(parts):
            if parts > 1:
                span = pl.ds(part * rows, rows)
                copies[name, part] = pltpu.make_async_copy(src.at[span], dst.at[span], sems.at[sem])
            else:
                copies[name, part] = pltpu.make_async_copy(src, dst, sems.at[sem])
            copies[name, part].start()
            sem += 1

    for name in ("hidden", "in_gain", "q_gain", "k_gain"):
        copies[name, 0].wait()
    states = hidden[...].astype(F32)
    mean_sq = jnp.mean(states * states, axis=-1, keepdims=True)
    normed = (states * lax.rsqrt(mean_sq + 1e-06) * in_gain[...].astype(F32).reshape(1, width)).astype(BF16)

    depth = width // qkv_parts
    projected = None
    for part in range(qkv_parts):
        copies["qkv", part].wait()
        term = jnp.dot(
            normed[:, part * depth : (part + 1) * depth],
            qkv[part * depth : (part + 1) * depth, :],
            preferred_element_type=F32,
        )
        projected = term if projected is None else projected + term

    cosine = cos_ref[...]
    sine = sin_ref[...]

    def norm_rotate(block, gain):
        mean = jnp.mean(block * block, axis=-1, keepdims=True)
        block = block * lax.rsqrt(mean + 1e-06) * gain
        swapped = jnp.concatenate([block[:, HEAD // 2 :], block[:, : HEAD // 2]], axis=-1)
        return block * cosine + swapped * sine

    q_scale = q_gain[...].astype(F32).reshape(1, HEAD)
    k_scale = k_gain[...].astype(F32).reshape(1, HEAD)
    queries = jnp.concatenate(
        [norm_rotate(projected[:, j * HEAD : (j + 1) * HEAD], q_scale) for j in range(GROUP)], axis=0
    ).astype(BF16)
    blank = jnp.zeros((ROWS - STEPS, HEAD), F32)
    keys_new = jnp.concatenate(
        [norm_rotate(projected[:, GROUP * HEAD : (GROUP + 1) * HEAD], k_scale), blank],
        axis=0,
    ).astype(BF16)
    values_new = jnp.concatenate([projected[:, (GROUP + 1) * HEAD :], blank], axis=0).astype(BF16)

    length = length_ref[0]
    scale = 1.0 / jnp.sqrt(F32(HEAD))
    contract = (((1,), (1,)), ((), ()))
    new = lax.dot_general(queries, keys_new, contract, preferred_element_type=F32) * scale
    row = lax.broadcasted_iota(jnp.int32, (ROWS, ROWS), 0) % STEPS
    step_ok = lax.broadcasted_iota(jnp.int32, (ROWS, ROWS), 1) <= row
    new = jnp.where(step_ok, new, -1e30)
    top = jnp.max(new, axis=-1, keepdims=True)
    span = slots // key_parts
    for part in range(key_parts):
        copies["keys", part].wait()
        score = lax.dot_general(
            queries, keys[part * span : (part + 1) * span, :], contract, preferred_element_type=F32
        ) * scale
        slot = lax.broadcasted_iota(jnp.int32, (ROWS, span), 1) + part * span
        score = jnp.where(slot < length, score, -1e30)
        scores[:, part * span : (part + 1) * span] = score
        top = jnp.maximum(top, jnp.max(score, axis=-1, keepdims=True))
    exp_new = jnp.where(step_ok, jnp.exp(new - top), 0.0)
    total = jnp.sum(exp_new, axis=-1, keepdims=True)
    for part in range(key_parts):
        exp_old = jnp.exp(scores[:, part * span : (part + 1) * span] - top)
        scores[:, part * span : (part + 1) * span] = exp_old
        total = total + jnp.sum(exp_old, axis=-1, keepdims=True)
    weight_new = (exp_new / total).astype(BF16)
    mixed = jnp.dot(weight_new, values_new, preferred_element_type=F32)
    span = slots // value_parts
    for part in range(value_parts):
        copies["values", part].wait()
        weight = (scores[:, part * span : (part + 1) * span] / total).astype(BF16)
        mixed = mixed + jnp.dot(
            weight, values[part * span : (part + 1) * span, :], preferred_element_type=F32
        )
    heads = jnp.concatenate([mixed[j * STEPS : (j + 1) * STEPS, :] for j in range(GROUP)], axis=-1)
    heads = heads.astype(BF16)
    partial = None
    depth = wout.shape[0] // out_parts
    for part in range(out_parts):
        copies["out", part].wait()
        term = jnp.dot(
            heads[:, part * depth : (part + 1) * depth],
            wout[part * depth : (part + 1) * depth, :],
            preferred_element_type=F32,
        )
        partial = term if partial is None else partial + term
    for peer in range(partial_ref.shape[0]):
        partial_ref[peer] = partial.astype(BF16)


def attention(hidden, in_gain, old_qkv, old_out, q_gain, k_gain, cache_keys, stored_values, cache_lengths, tp):
    width = hidden.shape[-1]
    slots = cache_keys.shape[1]
    cosine, sine = rope_tables(cache_lengths)
    vmem = pl.BlockSpec(memory_space=pltpu.VMEM)
    hbm = pl.BlockSpec(memory_space=pltpu.HBM)
    return pl.pallas_call(
        attention_kernel,
        out_shape=jax.ShapeDtypeStruct((tp, STEPS, width), BF16),
        in_specs=[pl.BlockSpec(memory_space=pltpu.SMEM)] + [vmem] * 2 + [hbm] * 8,
        out_specs=vmem,
        scratch_shapes=[
            pltpu.VMEM((STEPS, width), BF16),
            pltpu.VMEM(in_gain.shape, BF16),
            pltpu.VMEM(q_gain.shape, BF16),
            pltpu.VMEM(k_gain.shape, BF16),
            pltpu.VMEM(old_qkv.shape, BF16),
            pltpu.VMEM((slots, HEAD), BF16),
            pltpu.VMEM((slots, HEAD), BF16),
            pltpu.VMEM(old_out.shape, BF16),
            pltpu.VMEM((ROWS, slots), F32),
            pltpu.SemaphoreType.DMA((17,)),
        ],
        compiler_params=pltpu.CompilerParams(vmem_limit_bytes=60 * 1024 * 1024),
        cost_estimate=pl.CostEstimate(flops=120_000_000, bytes_accessed=17_400_000, transcendentals=140_000),
        name="attention",
    )(
        cache_lengths, cosine, sine, hidden.reshape(STEPS, width), in_gain, q_gain, k_gain, old_qkv,
        cache_keys.reshape(slots, HEAD),
        stored_values.reshape(slots, HEAD), old_out,
    )


def place(pieces, shape, previous=None):
    slots = jnp.stack([piece[3] for piece in pieces]).astype(jnp.int32)
    arrays = []
    for piece in pieces:
        if all(piece[0] is not array for array in arrays):
            arrays.append(piece[0])
    which = [next(i for i, array in enumerate(arrays) if array is piece[0]) for piece in pieces]
    count = len(arrays)

    def kernel(slots_ref, *refs):
        sources, out, sems = refs[:count], refs[-2], refs[-1]
        copies = []
        for i, (_, first, size, _, start) in enumerate(pieces):
            copy = pltpu.make_async_copy(
                sources[which[i]].at[pl.ds(first, size)],
                out.at[slots_ref[i], pl.ds(start, size)],
                sems.at[i],
            )
            copy.start()
            copies.append(copy)
        for copy in copies:
            copy.wait()

    operands = [slots] + arrays + ([] if previous is None else [previous])
    size = sum(array.size for array in arrays) * 2
    return pl.pallas_call(
        kernel,
        out_shape=jax.ShapeDtypeStruct(shape, BF16),
        in_specs=[pl.BlockSpec(memory_space=pltpu.SMEM)]
        + [pl.BlockSpec(memory_space=pltpu.VMEM)] * count
        + [pl.BlockSpec(memory_space=pl.ANY)] * (previous is not None),
        out_specs=pl.BlockSpec(memory_space=pl.ANY),
        scratch_shapes=[pltpu.SemaphoreType.DMA((len(pieces),))],
        compiler_params=pltpu.CompilerParams(vmem_limit_bytes=16 * 1024 * 1024),
        input_output_aliases={} if previous is None else {len(operands) - 1: 0},
        cost_estimate=pl.CostEstimate(flops=0, bytes_accessed=2 * size, transcendentals=0),
        name="place",
    )(*operands)


def swap(array, axis):
    return lax.ppermute(array, axis, [(0, 1), (1, 0)])


def ring(array):
    pairs = []
    for x in range(4):
        pairs += [(2 * x, (x + 1) % 4 * 2), (2 * x + 1, (x + 3) % 4 * 2 + 1)]
    return lax.ppermute(array, ("x", "core"), pairs)


def body(
    hidden, in_gain, old_qkv, old_out, q_gain, k_gain, cache_keys, stored_values, cache_lengths, new_qkv
):
    rows, columns = new_qkv.shape
    tp = lax.axis_size(TP)
    rep = lax.axis_size(REP)
    z, x, core = lax.axis_index("z_hi"), lax.axis_index("x"), lax.axis_index("core")
    back = 2 * core + 3

    def slot(dz, dx, dc):
        return ((z + dz) % 2 * 4 + (x + dx) % 4) * 2 + (core + dc) % 2

    blocks = new_qkv.reshape(rows, tp, columns // tp).transpose(1, 0, 2)
    own = lax.all_to_all(blocks, TP, split_axis=0, concat_axis=0, tiled=True)
    partial = attention(
        hidden, in_gain, old_qkv, old_out, q_gain, k_gain, cache_keys, stored_values, cache_lengths, tp
    )
    own, partial = lax.optimization_barrier((own, partial))
    shape = (rep, tp, rows, columns // tp)

    other = swap(own, "z_hi")
    core_own = swap(own, "core")
    near = ring(own)
    near_pair = ring(core_own)
    near, partial = lax.optimization_barrier((near, partial))
    terms = lax.all_to_all(partial, TP, split_axis=0, concat_axis=0, tiled=True)
    far = ring(near)
    core_near = swap(near, "core")
    other_near_pair = swap(near_pair, "z_hi")
    core_near_pair = swap(near_pair, "core")
    core_far = swap(far, "core")
    other_near = ring(other)
    core_other = swap(other, "core")
    out = place(
        [
            (own, 0, tp, slot(0, 0, 0), 0),
            (core_own, 0, tp, slot(0, 0, 1), 0),
            (near, 0, tp, slot(0, back, 0), 0),
            (core_near, 0, tp, slot(0, -back, 1), 0),
            (near_pair, 0, tp, slot(0, back, 1), 0),
            (core_near_pair, 0, tp, slot(0, -back, 0), 0),
        ],
        shape,
    )
    out, terms, other_near = lax.optimization_barrier((out, terms, other_near))
    other_far = ring(other_near)
    core_other_near = swap(other_near, "core")
    attended = terms[0].astype(F32)
    for peer in range(1, tp):
        attended = attended + terms[peer].astype(F32)
    attended = attended.astype(BF16)
    out = place(
        [
            (far, 0, tp, slot(0, 2, 0), 0),
            (core_far, 0, tp, slot(0, 2, 1), 0),
            (other, 0, tp, slot(1, 0, 0), 0),
            (core_other, 0, tp, slot(1, 0, 1), 0),
            (other_near, 0, tp, slot(1, back, 0), 0),
            (core_other_near, 0, tp, slot(1, -back, 1), 0),
        ],
        shape,
        out,
    )
    out, attended, other_near_pair, other_far = lax.optimization_barrier((out, attended, other_near_pair, other_far))
    core_other_near_pair = swap(other_near_pair, "core")
    core_other_far = swap(other_far, "core")
    out = place(
        [
            (other_near_pair, 0, tp, slot(1, back, 1), 0),
            (other_far, 0, tp, slot(1, 2, 0), 0),
            (core_other_near_pair, 0, tp, slot(1, -back, 0), 0),
            (core_other_far, 0, tp, slot(1, 2, 1), 0),
        ],
        shape,
        out,
    )
    return attended.reshape(hidden.shape), out.reshape(rep * tp * rows, columns // tp)


def solution(mesh):
    fine = jax.sharding.Mesh(mesh.devices.reshape(2, 4, 2, mesh.shape["tp"]), REP + (TP,))
    in_specs = (
        P(REP, None, None),
        P(),
        P(None, TP),
        P(TP, None),
        P(),
        P(),
        P(REP, None, TP, None),
        P(REP, None, TP, None),
        P(REP),
        P(REP + (TP,), None),
    )
    out_specs = (P(REP, None, None), P(None, TP))
    return jax.shard_map(body, mesh=fine, in_specs=in_specs, out_specs=out_specs, check_vma=False)
```

```python
import jax
import jax.numpy as jnp
from jax import lax
from jax.experimental import pallas as pl
from jax.experimental.pallas import tpu as pltpu
from jax.sharding import PartitionSpec as P

BF16 = jnp.bfloat16
F32 = jnp.float32
STEPS = 4
GROUP = 4
HEAD = 128
ROWS = STEPS * GROUP
REP = ("z_hi", "x", "core")
TP = "tp"


def rope_tables(cache_lengths):
    half = HEAD // 2
    frequency = 1000000.0 ** (-(jnp.arange(half).astype(F32) * 2.0 / HEAD))
    positions = (cache_lengths[:, None] + jnp.arange(STEPS)[None, :]).astype(F32)
    angles = positions[0, :, None] * frequency
    cosine = jnp.cos(angles)
    sine = jnp.sin(angles)
    return jnp.concatenate([cosine, cosine], axis=-1), jnp.concatenate([-sine, sine], axis=-1)


def attention_kernel(
    length_ref, cos_ref, sin_ref,
    hidden_hbm, in_gain_hbm, q_gain_hbm, k_gain_hbm, qkv_hbm, keys_hbm, values_hbm, out_hbm,
    partial_ref,
    hidden, in_gain, q_gain, k_gain, qkv, keys, values, wout, scores, sems,
):
    width = qkv.shape[0]
    slots = keys.shape[0]
    qkv_parts, key_parts, value_parts, out_parts = 5, 2, 2, 4
    copies = {}
    sem = 0
    for name, src, dst, parts in (
        ("hidden", hidden_hbm, hidden, 1),
        ("in_gain", in_gain_hbm, in_gain, 1),
        ("q_gain", q_gain_hbm, q_gain, 1),
        ("k_gain", k_gain_hbm, k_gain, 1),
        ("qkv", qkv_hbm, qkv, qkv_parts),
        ("keys", keys_hbm, keys, key_parts),
        ("values", values_hbm, values, value_parts),
        ("out", out_hbm, wout, out_parts),
    ):
        rows = src.shape[0] // parts
        for part in range(parts):
            if parts > 1:
                span = pl.ds(part * rows, rows)
                copies[name, part] = pltpu.make_async_copy(src.at[span], dst.at[span], sems.at[sem])
            else:
                copies[name, part] = pltpu.make_async_copy(src, dst, sems.at[sem])
            copies[name, part].start()
            sem += 1

    for name in ("hidden", "in_gain", "q_gain", "k_gain"):
        copies[name, 0].wait()
    states = hidden[...].astype(F32)
    mean_sq = jnp.mean(states * states, axis=-1, keepdims=True)
    normed = (states * lax.rsqrt(mean_sq + 1e-06) * in_gain[...].astype(F32).reshape(1, width)).astype(BF16)

    depth = width // qkv_parts
    projected = None
    for part in range(qkv_parts):
        copies["qkv", part].wait()
        term = jnp.dot(
            normed[:, part * depth : (part + 1) * depth],
            qkv[part * depth : (part + 1) * depth, :],
            preferred_element_type=F32,
        )
        projected = term if projected is None else projected + term

    cosine = cos_ref[...]
    sine = sin_ref[...]

    def norm_rotate(block, gain):
        mean = jnp.mean(block * block, axis=-1, keepdims=True)
        block = block * lax.rsqrt(mean + 1e-06) * gain
        swapped = jnp.concatenate([block[:, HEAD // 2 :], block[:, : HEAD // 2]], axis=-1)
        return block * cosine + swapped * sine

    q_scale = q_gain[...].astype(F32).reshape(1, HEAD)
    k_scale = k_gain[...].astype(F32).reshape(1, HEAD)
    queries = jnp.concatenate(
        [norm_rotate(projected[:, j * HEAD : (j + 1) * HEAD], q_scale) for j in range(GROUP)], axis=0
    ).astype(BF16)
    blank = jnp.zeros((ROWS - STEPS, HEAD), F32)
    keys_new = jnp.concatenate(
        [norm_rotate(projected[:, GROUP * HEAD : (GROUP + 1) * HEAD], k_scale), blank],
        axis=0,
    ).astype(BF16)
    values_new = jnp.concatenate([projected[:, (GROUP + 1) * HEAD :], blank], axis=0).astype(BF16)

    length = length_ref[0]
    scale = 1.0 / jnp.sqrt(F32(HEAD))
    contract = (((1,), (1,)), ((), ()))
    new = lax.dot_general(queries, keys_new, contract, preferred_element_type=F32) * scale
    row = lax.broadcasted_iota(jnp.int32, (ROWS, ROWS), 0) % STEPS
    step_ok = lax.broadcasted_iota(jnp.int32, (ROWS, ROWS), 1) <= row
    new = jnp.where(step_ok, new, -1e30)
    top = jnp.max(new, axis=-1, keepdims=True)
    span = slots // key_parts
    for part in range(key_parts):
        copies["keys", part].wait()
        score = lax.dot_general(
            queries, keys[part * span : (part + 1) * span, :], contract, preferred_element_type=F32
        ) * scale
        slot = lax.broadcasted_iota(jnp.int32, (ROWS, span), 1) + part * span
        score = jnp.where(slot < length, score, -1e30)
        scores[:, part * span : (part + 1) * span] = score
        top = jnp.maximum(top, jnp.max(score, axis=-1, keepdims=True))
    exp_new = jnp.where(step_ok, jnp.exp(new - top), 0.0)
    total = jnp.sum(exp_new, axis=-1, keepdims=True)
    for part in range(key_parts):
        exp_old = jnp.exp(scores[:, part * span : (part + 1) * span] - top)
        scores[:, part * span : (part + 1) * span] = exp_old
        total = total + jnp.sum(exp_old, axis=-1, keepdims=True)
    weight_new = (exp_new / total).astype(BF16)
    mixed = jnp.dot(weight_new, values_new, preferred_element_type=F32)
    span = slots // value_parts
    for part in range(value_parts):
        copies["values", part].wait()
        weight = (scores[:, part * span : (part + 1) * span] / total).astype(BF16)
        mixed = mixed + jnp.dot(
            weight, values[part * span : (part + 1) * span, :], preferred_element_type=F32
        )
    heads = jnp.concatenate([mixed[j * STEPS : (j + 1) * STEPS, :] for j in range(GROUP)], axis=-1)
    heads = heads.astype(BF16)
    partial = None
    depth = wout.shape[0] // out_parts
    for part in range(out_parts):
        copies["out", part].wait()
        term = jnp.dot(
            heads[:, part * depth : (part + 1) * depth],
            wout[part * depth : (part + 1) * depth, :],
            preferred_element_type=F32,
        )
        partial = term if partial is None else partial + term
    for peer in range(partial_ref.shape[0]):
        partial_ref[peer] = partial.astype(BF16)


def attention(hidden, in_gain, old_qkv, old_out, q_gain, k_gain, cache_keys, stored_values, cache_lengths, tp):
    width = hidden.shape[-1]
    slots = cache_keys.shape[1]
    cosine, sine = rope_tables(cache_lengths)
    vmem = pl.BlockSpec(memory_space=pltpu.VMEM)
    hbm = pl.BlockSpec(memory_space=pltpu.HBM)
    return pl.pallas_call(
        attention_kernel,
        out_shape=jax.ShapeDtypeStruct((tp, STEPS, width), BF16),
        in_specs=[pl.BlockSpec(memory_space=pltpu.SMEM)] + [vmem] * 2 + [hbm] * 8,
        out_specs=vmem,
        scratch_shapes=[
            pltpu.VMEM((STEPS, width), BF16),
            pltpu.VMEM(in_gain.shape, BF16),
            pltpu.VMEM(q_gain.shape, BF16),
            pltpu.VMEM(k_gain.shape, BF16),
            pltpu.VMEM(old_qkv.shape, BF16),
            pltpu.VMEM((slots, HEAD), BF16),
            pltpu.VMEM((slots, HEAD), BF16),
            pltpu.VMEM(old_out.shape, BF16),
            pltpu.VMEM((ROWS, slots), F32),
            pltpu.SemaphoreType.DMA((17,)),
        ],
        compiler_params=pltpu.CompilerParams(vmem_limit_bytes=60 * 1024 * 1024),
        cost_estimate=pl.CostEstimate(flops=120_000_000, bytes_accessed=17_400_000, transcendentals=140_000),
        name="attention",
    )(
        cache_lengths, cosine, sine, hidden.reshape(STEPS, width), in_gain, q_gain, k_gain, old_qkv,
        cache_keys.reshape(slots, HEAD),
        stored_values.reshape(slots, HEAD), old_out,
    )


def place(pieces, shape, previous=None):
    slots = jnp.stack([piece[3] for piece in pieces]).astype(jnp.int32)
    arrays = []
    for piece in pieces:
        if all(piece[0] is not array for array in arrays):
            arrays.append(piece[0])
    which = [next(i for i, array in enumerate(arrays) if array is piece[0]) for piece in pieces]
    count = len(arrays)

    def kernel(slots_ref, *refs):
        sources, out, sems = refs[:count], refs[-2], refs[-1]
        copies = []
        for i, (_, first, size, _, start) in enumerate(pieces):
            copy = pltpu.make_async_copy(
                sources[which[i]].at[pl.ds(first, size)],
                out.at[slots_ref[i], pl.ds(start, size)],
                sems.at[i],
            )
            copy.start()
            copies.append(copy)
        for copy in copies:
            copy.wait()

    operands = [slots] + arrays + ([] if previous is None else [previous])
    size = sum(array.size for array in arrays) * 2
    return pl.pallas_call(
        kernel,
        out_shape=jax.ShapeDtypeStruct(shape, BF16),
        in_specs=[pl.BlockSpec(memory_space=pltpu.SMEM)]
        + [pl.BlockSpec(memory_space=pltpu.VMEM)] * count
        + [pl.BlockSpec(memory_space=pl.ANY)] * (previous is not None),
        out_specs=pl.BlockSpec(memory_space=pl.ANY),
        scratch_shapes=[pltpu.SemaphoreType.DMA((len(pieces),))],
        compiler_params=pltpu.CompilerParams(vmem_limit_bytes=16 * 1024 * 1024),
        input_output_aliases={} if previous is None else {len(operands) - 1: 0},
        cost_estimate=pl.CostEstimate(flops=0, bytes_accessed=2 * size, transcendentals=0),
        name="place",
    )(*operands)


def swap(array, axis):
    return lax.ppermute(array, axis, [(0, 1), (1, 0)])


def ring(array):
    pairs = []
    for x in range(4):
        pairs += [(2 * x, (x + 1) % 4 * 2), (2 * x + 1, (x + 3) % 4 * 2 + 1)]
    return lax.ppermute(array, ("x", "core"), pairs)


def body(
    hidden, in_gain, old_qkv, old_out, q_gain, k_gain, cache_keys, stored_values, cache_lengths, new_qkv
):
    rows, columns = new_qkv.shape
    tp = lax.axis_size(TP)
    rep = lax.axis_size(REP)
    z, x, core = lax.axis_index("z_hi"), lax.axis_index("x"), lax.axis_index("core")
    back = 2 * core + 3

    def slot(dz, dx, dc):
        return ((z + dz) % 2 * 4 + (x + dx) % 4) * 2 + (core + dc) % 2

    blocks = new_qkv.reshape(rows, tp, columns // tp).transpose(1, 0, 2)
    own = lax.all_to_all(blocks, TP, split_axis=0, concat_axis=0, tiled=True)
    partial = attention(
        hidden, in_gain, old_qkv, old_out, q_gain, k_gain, cache_keys, stored_values, cache_lengths, tp
    )
    own, partial = lax.optimization_barrier((own, partial))
    shape = (rep, tp, rows, columns // tp)

    other = swap(own, "z_hi")
    core_own = swap(own, "core")
    near = ring(own)
    near_pair = ring(core_own)
    out = place(
        [
            (own, 0, tp, slot(0, 0, 0), 0),
            (core_own, 0, tp, slot(0, 0, 1), 0),
            (near, 0, tp, slot(0, back, 0), 0),
        ],
        shape,
    )
    far = ring(near)
    core_near = swap(near, "core")
    core_near_pair = swap(near_pair, "core")
    core_far = swap(far, "core")
    other_far = swap(far, "z_hi")
    other, near_pair, out = lax.optimization_barrier((other, near_pair, out))
    other_near = ring(other)
    core_other = swap(other, "core")
    core_other, partial = lax.optimization_barrier((core_other, partial))
    terms = lax.all_to_all(partial, TP, split_axis=0, concat_axis=0, tiled=True)
    other_near_pair = ring(core_other)
    core_other_near = swap(other_near, "core")
    out = place(
        [
            (near_pair, 0, tp, slot(0, back, 1), 0),
            (core_near, 0, tp, slot(0, -back, 1), 0),
            (core_near_pair, 0, tp, slot(0, -back, 0), 0),
            (other, 0, tp, slot(1, 0, 0), 0),
            (far, 0, tp, slot(0, 2, 0), 0),
            (core_far, 0, tp, slot(0, 2, 1), 0),
            (core_other, 0, tp, slot(1, 0, 1), 0),
            (other_near, 0, tp, slot(1, back, 0), 0),
            (core_other_near, 0, tp, slot(1, -back, 1), 0),
        ],
        shape,
        out,
    )
    out, other_near_pair, other_far = lax.optimization_barrier((out, other_near_pair, other_far))
    core_other_near_pair = swap(other_near_pair, "core")
    core_other_far = swap(other_far, "core")
    attended = terms[0].astype(F32)
    for peer in range(1, tp):
        attended = attended + terms[peer].astype(F32)
    attended = attended.astype(BF16)
    out = place(
        [
            (other_near_pair, 0, tp, slot(1, back, 1), 0),
            (other_far, 0, tp, slot(1, 2, 0), 0),
            (core_other_near_pair, 0, tp, slot(1, -back, 0), 0),
            (core_other_far, 0, tp, slot(1, 2, 1), 0),
        ],
        shape,
        out,
    )
    return attended.reshape(hidden.shape), out.reshape(rep * tp * rows, columns // tp)


def solution(mesh):
    fine = jax.sharding.Mesh(mesh.devices.reshape(2, 4, 2, mesh.shape["tp"]), REP + (TP,))
    in_specs = (
        P(REP, None, None),
        P(),
        P(None, TP),
        P(TP, None),
        P(),
        P(),
        P(REP, None, TP, None),
        P(REP, None, TP, None),
        P(REP),
        P(REP + (TP,), None),
    )
    out_specs = (P(REP, None, None), P(None, TP))
    return jax.shard_map(body, mesh=fine, in_specs=in_specs, out_specs=out_specs, check_vma=False)
```

```python
import jax
import jax.numpy as jnp
from jax import lax
from jax.experimental import pallas as pl
from jax.experimental.pallas import tpu as pltpu
from jax.sharding import PartitionSpec as P

BF16 = jnp.bfloat16
F32 = jnp.float32
STEPS = 4
GROUP = 4
HEAD = 128
ROWS = STEPS * GROUP
REP = ("z_hi", "x", "core")
TP = ("y", "z_lo")


def rope_tables(cache_lengths):
    half = HEAD // 2
    frequency = 1000000.0 ** (-(jnp.arange(half).astype(F32) * 2.0 / HEAD))
    positions = (cache_lengths[:, None] + jnp.arange(STEPS)[None, :]).astype(F32)
    angles = positions[0, :, None] * frequency
    cosine = jnp.cos(angles)
    sine = jnp.sin(angles)
    return jnp.concatenate([cosine, cosine], axis=-1), jnp.concatenate([-sine, sine], axis=-1)


def attention_kernel(
    length_ref, cos_ref, sin_ref,
    hidden_hbm, in_gain_hbm, q_gain_hbm, k_gain_hbm, qkv_hbm, keys_hbm, values_hbm, out_hbm,
    partial_ref,
    hidden, in_gain, q_gain, k_gain, qkv, keys, values, wout, scores, sems,
):
    width = qkv.shape[0]
    slots = keys.shape[0]
    qkv_parts, key_parts, value_parts, out_parts = 5, 2, 2, 4
    copies = {}
    sem = 0
    for name, src, dst, parts in (
        ("hidden", hidden_hbm, hidden, 1),
        ("in_gain", in_gain_hbm, in_gain, 1),
        ("q_gain", q_gain_hbm, q_gain, 1),
        ("k_gain", k_gain_hbm, k_gain, 1),
        ("qkv", qkv_hbm, qkv, qkv_parts),
        ("keys", keys_hbm, keys, key_parts),
        ("values", values_hbm, values, value_parts),
        ("out", out_hbm, wout, out_parts),
    ):
        rows = src.shape[0] // parts
        for part in range(parts):
            if parts > 1:
                span = pl.ds(part * rows, rows)
                copies[name, part] = pltpu.make_async_copy(src.at[span], dst.at[span], sems.at[sem])
            else:
                copies[name, part] = pltpu.make_async_copy(src, dst, sems.at[sem])
            copies[name, part].start()
            sem += 1

    for name in ("hidden", "in_gain", "q_gain", "k_gain"):
        copies[name, 0].wait()
    states = hidden[...].astype(F32)
    mean_sq = jnp.mean(states * states, axis=-1, keepdims=True)
    normed = (states * lax.rsqrt(mean_sq + 1e-06) * in_gain[...].astype(F32).reshape(1, width)).astype(BF16)

    depth = width // qkv_parts
    projected = None
    for part in range(qkv_parts):
        copies["qkv", part].wait()
        term = jnp.dot(
            normed[:, part * depth : (part + 1) * depth],
            qkv[part * depth : (part + 1) * depth, :],
            preferred_element_type=F32,
        )
        projected = term if projected is None else projected + term

    cosine = cos_ref[...]
    sine = sin_ref[...]

    def norm_rotate(block, gain):
        mean = jnp.mean(block * block, axis=-1, keepdims=True)
        block = block * lax.rsqrt(mean + 1e-06) * gain
        swapped = jnp.concatenate([block[:, HEAD // 2 :], block[:, : HEAD // 2]], axis=-1)
        return block * cosine + swapped * sine

    q_scale = q_gain[...].astype(F32).reshape(1, HEAD)
    k_scale = k_gain[...].astype(F32).reshape(1, HEAD)
    queries = jnp.concatenate(
        [norm_rotate(projected[:, j * HEAD : (j + 1) * HEAD], q_scale) for j in range(GROUP)], axis=0
    ).astype(BF16)
    blank = jnp.zeros((ROWS - STEPS, HEAD), F32)
    keys_new = jnp.concatenate(
        [norm_rotate(projected[:, GROUP * HEAD : (GROUP + 1) * HEAD], k_scale), blank],
        axis=0,
    ).astype(BF16)
    values_new = jnp.concatenate([projected[:, (GROUP + 1) * HEAD :], blank], axis=0).astype(BF16)

    length = length_ref[0]
    scale = 1.0 / jnp.sqrt(F32(HEAD))
    contract = (((1,), (1,)), ((), ()))
    new = lax.dot_general(queries, keys_new, contract, preferred_element_type=F32) * scale
    row = lax.broadcasted_iota(jnp.int32, (ROWS, ROWS), 0) % STEPS
    step_ok = lax.broadcasted_iota(jnp.int32, (ROWS, ROWS), 1) <= row
    new = jnp.where(step_ok, new, -1e30)
    top = jnp.max(new, axis=-1, keepdims=True)
    span = slots // key_parts
    for part in range(key_parts):
        copies["keys", part].wait()
        score = lax.dot_general(
            queries, keys[part * span : (part + 1) * span, :], contract, preferred_element_type=F32
        ) * scale
        slot = lax.broadcasted_iota(jnp.int32, (ROWS, span), 1) + part * span
        score = jnp.where(slot < length, score, -1e30)
        scores[:, part * span : (part + 1) * span] = score
        top = jnp.maximum(top, jnp.max(score, axis=-1, keepdims=True))
    exp_new = jnp.where(step_ok, jnp.exp(new - top), 0.0)
    total = jnp.sum(exp_new, axis=-1, keepdims=True)
    for part in range(key_parts):
        exp_old = jnp.exp(scores[:, part * span : (part + 1) * span] - top)
        scores[:, part * span : (part + 1) * span] = exp_old
        total = total + jnp.sum(exp_old, axis=-1, keepdims=True)
    weight_new = (exp_new / total).astype(BF16)
    mixed = jnp.dot(weight_new, values_new, preferred_element_type=F32)
    span = slots // value_parts
    for part in range(value_parts):
        copies["values", part].wait()
        weight = (scores[:, part * span : (part + 1) * span] / total).astype(BF16)
        mixed = mixed + jnp.dot(
            weight, values[part * span : (part + 1) * span, :], preferred_element_type=F32
        )
    heads = jnp.concatenate([mixed[j * STEPS : (j + 1) * STEPS, :] for j in range(GROUP)], axis=-1)
    heads = heads.astype(BF16)
    partial = None
    depth = wout.shape[0] // out_parts
    for part in range(out_parts):
        copies["out", part].wait()
        term = jnp.dot(
            heads[:, part * depth : (part + 1) * depth],
            wout[part * depth : (part + 1) * depth, :],
            preferred_element_type=F32,
        )
        partial = term if partial is None else partial + term
    partial_ref[...] = partial.astype(BF16)


def attention(hidden, in_gain, old_qkv, old_out, q_gain, k_gain, cache_keys, stored_values, cache_lengths):
    width = hidden.shape[-1]
    slots = cache_keys.shape[1]
    cosine, sine = rope_tables(cache_lengths)
    vmem = pl.BlockSpec(memory_space=pltpu.VMEM)
    hbm = pl.BlockSpec(memory_space=pltpu.HBM)
    return pl.pallas_call(
        attention_kernel,
        out_shape=jax.ShapeDtypeStruct((STEPS, width), BF16),
        in_specs=[pl.BlockSpec(memory_space=pltpu.SMEM)] + [vmem] * 2 + [hbm] * 8,
        out_specs=vmem,
        scratch_shapes=[
            pltpu.VMEM((STEPS, width), BF16),
            pltpu.VMEM(in_gain.shape, BF16),
            pltpu.VMEM(q_gain.shape, BF16),
            pltpu.VMEM(k_gain.shape, BF16),
            pltpu.VMEM(old_qkv.shape, BF16),
            pltpu.VMEM((slots, HEAD), BF16),
            pltpu.VMEM((slots, HEAD), BF16),
            pltpu.VMEM(old_out.shape, BF16),
            pltpu.VMEM((ROWS, slots), F32),
            pltpu.SemaphoreType.DMA((17,)),
        ],
        compiler_params=pltpu.CompilerParams(vmem_limit_bytes=60 * 1024 * 1024),
        cost_estimate=pl.CostEstimate(flops=120_000_000, bytes_accessed=17_400_000, transcendentals=140_000),
        name="attention",
    )(
        cache_lengths, cosine, sine, hidden.reshape(STEPS, width), in_gain, q_gain, k_gain, old_qkv,
        cache_keys.reshape(slots, HEAD),
        stored_values.reshape(slots, HEAD), old_out,
    )


def place(pieces, shape, previous=None):
    slots = jnp.stack([piece[3] for piece in pieces]).astype(jnp.int32)
    arrays = []
    for piece in pieces:
        if all(piece[0] is not array for array in arrays):
            arrays.append(piece[0])
    which = [next(i for i, array in enumerate(arrays) if array is piece[0]) for piece in pieces]
    count = len(arrays)

    def kernel(slots_ref, *refs):
        sources, out, sems = refs[:count], refs[-2], refs[-1]
        copies = []
        for i, (_, first, size, _, start) in enumerate(pieces):
            copy = pltpu.make_async_copy(
                sources[which[i]].at[pl.ds(first, size)],
                out.at[slots_ref[i], pl.ds(start, size)],
                sems.at[i],
            )
            copy.start()
            copies.append(copy)
        for copy in copies:
            copy.wait()

    operands = [slots] + arrays + ([] if previous is None else [previous])
    size = sum(array.size for array in arrays) * 2
    return pl.pallas_call(
        kernel,
        out_shape=jax.ShapeDtypeStruct(shape, BF16),
        in_specs=[pl.BlockSpec(memory_space=pltpu.SMEM)]
        + [pl.BlockSpec(memory_space=pltpu.VMEM)] * count
        + [pl.BlockSpec(memory_space=pl.ANY)] * (previous is not None),
        out_specs=pl.BlockSpec(memory_space=pl.ANY),
        scratch_shapes=[pltpu.SemaphoreType.DMA((len(pieces),))],
        compiler_params=pltpu.CompilerParams(vmem_limit_bytes=16 * 1024 * 1024),
        input_output_aliases={} if previous is None else {len(operands) - 1: 0},
        cost_estimate=pl.CostEstimate(flops=0, bytes_accessed=2 * size, transcendentals=0),
        name="place",
    )(*operands)


def swap(array, axis):
    return lax.ppermute(array, axis, [(0, 1), (1, 0)])


def ring(array):
    pairs = []
    for x in range(4):
        pairs += [(2 * x, (x + 1) % 4 * 2), (2 * x + 1, (x + 3) % 4 * 2 + 1)]
    return lax.ppermute(array, ("x", "core"), pairs)


def body(
    hidden, in_gain, old_qkv, old_out, q_gain, k_gain, cache_keys, stored_values, cache_lengths, new_qkv
):
    rows, columns = new_qkv.shape
    tp = lax.axis_size(TP)
    rep = lax.axis_size(REP)
    z, x, core = lax.axis_index("z_hi"), lax.axis_index("x"), lax.axis_index("core")
    back = 2 * core + 3

    def slot(dz, dx, dc):
        return ((z + dz) % 2 * 4 + (x + dx) % 4) * 2 + (core + dc) % 2

    blocks = new_qkv.reshape(rows, tp, columns // tp).transpose(1, 0, 2)
    own = lax.all_to_all(blocks, TP, split_axis=0, concat_axis=0, tiled=True)
    partial = attention(
        hidden, in_gain, old_qkv, old_out, q_gain, k_gain, cache_keys, stored_values, cache_lengths
    )
    own, partial = lax.optimization_barrier((own, partial))
    shape = (rep, tp, rows, columns // tp)

    other = swap(own, "z_hi")
    core_own = swap(own, "core")
    near = ring(own)
    near, partial = lax.optimization_barrier((near, partial))
    pair = swap(partial, "z_lo")
    partial = (partial.astype(F32) + pair.astype(F32)).astype(BF16)
    partial = jnp.broadcast_to(partial[None], (4,) + partial.shape)
    near_pair = ring(core_own)
    out = place(
        [
            (own, 0, tp, slot(0, 0, 0), 0),
            (core_own, 0, tp, slot(0, 0, 1), 0),
            (near, 0, tp, slot(0, back, 0), 0),
        ],
        shape,
    )
    far = ring(near)
    core_near = swap(near, "core")
    core_near_pair = swap(near_pair, "core")
    core_far = swap(far, "core")
    other_far = swap(far, "z_hi")
    other, near_pair, out = lax.optimization_barrier((other, near_pair, out))
    other_near = ring(other)
    core_other = swap(other, "core")
    core_other, partial = lax.optimization_barrier((core_other, partial))
    terms = lax.all_to_all(partial, "y", split_axis=0, concat_axis=0, tiled=True)
    other_near_pair = ring(core_other)
    out = place(
        [
            (near_pair, 0, tp, slot(0, back, 1), 0),
            (core_near, 0, tp, slot(0, -back, 1), 0),
            (core_near_pair, 0, tp, slot(0, -back, 0), 0),
            (other, 0, tp, slot(1, 0, 0), 0),
            (core_other, 0, tp, slot(1, 0, 1), 0),
            (far, 0, tp, slot(0, 2, 0), 0),
            (core_far, 0, tp, slot(0, 2, 1), 0),
        ],
        shape,
        out,
    )
    other_near, other_near_pair, other_far, out = lax.optimization_barrier((other_near, other_near_pair, other_far, out))
    core_other_near = swap(other_near, "core")
    core_other_near_pair = swap(other_near_pair, "core")
    core_other_far = swap(other_far, "core")
    attended = terms[0].astype(F32)
    for peer in range(1, 4):
        attended = attended + terms[peer].astype(F32)
    attended = attended.astype(BF16)
    out = place(
        [
            (other_near, 0, tp, slot(1, back, 0), 0),
            (core_other_near, 0, tp, slot(1, -back, 1), 0),
            (other_near_pair, 0, tp, slot(1, back, 1), 0),
            (core_other_near_pair, 0, tp, slot(1, -back, 0), 0),
            (other_far, 0, tp, slot(1, 2, 0), 0),
            (core_other_far, 0, tp, slot(1, 2, 1), 0),
        ],
        shape,
        out,
    )
    return attended.reshape(hidden.shape), out.reshape(rep * tp * rows, columns // tp)


def solution(mesh):
    fine = jax.sharding.Mesh(mesh.devices.reshape(2, 4, 2, 4, 2), REP + TP)
    in_specs = (
        P(REP, None, None),
        P(),
        P(None, TP),
        P(TP, None),
        P(),
        P(),
        P(REP, None, TP, None),
        P(REP, None, TP, None),
        P(REP),
        P(REP + TP, None),
    )
    out_specs = (P(REP, None, None), P(None, TP))
    return jax.shard_map(body, mesh=fine, in_specs=in_specs, out_specs=out_specs, check_vma=False)
```

```python
import jax
import jax.numpy as jnp
from jax import lax
from jax.experimental import pallas as pl
from jax.experimental.pallas import tpu as pltpu
from jax.sharding import PartitionSpec as P

BF16 = jnp.bfloat16
F32 = jnp.float32
STEPS = 4
GROUP = 4
HEAD = 128
ROWS = STEPS * GROUP
REP = ("z_hi", "x", "core")
TP = ("y", "z_lo")


def rope_tables(cache_lengths):
    half = HEAD // 2
    frequency = 1000000.0 ** (-(jnp.arange(half).astype(F32) * 2.0 / HEAD))
    positions = (cache_lengths[:, None] + jnp.arange(STEPS)[None, :]).astype(F32)
    angles = positions[0, :, None] * frequency
    cosine = jnp.cos(angles)
    sine = jnp.sin(angles)
    return jnp.concatenate([cosine, cosine], axis=-1), jnp.concatenate([-sine, sine], axis=-1)


def attention_kernel(
    length_ref, cos_ref, sin_ref,
    hidden_hbm, in_gain_hbm, q_gain_hbm, k_gain_hbm, qkv_hbm, keys_hbm, values_hbm, out_hbm,
    partial_ref,
    hidden, in_gain, q_gain, k_gain, qkv, keys, values, wout, scores, sems,
):
    width = qkv.shape[0]
    slots = keys.shape[0]
    qkv_parts, key_parts, value_parts, out_parts = 5, 2, 2, 4
    copies = {}
    sem = 0
    for name, src, dst, parts in (
        ("hidden", hidden_hbm, hidden, 1),
        ("in_gain", in_gain_hbm, in_gain, 1),
        ("q_gain", q_gain_hbm, q_gain, 1),
        ("k_gain", k_gain_hbm, k_gain, 1),
        ("qkv", qkv_hbm, qkv, qkv_parts),
        ("keys", keys_hbm, keys, key_parts),
        ("values", values_hbm, values, value_parts),
        ("out", out_hbm, wout, out_parts),
    ):
        rows = src.shape[0] // parts
        for part in range(parts):
            if parts > 1:
                span = pl.ds(part * rows, rows)
                copies[name, part] = pltpu.make_async_copy(src.at[span], dst.at[span], sems.at[sem])
            else:
                copies[name, part] = pltpu.make_async_copy(src, dst, sems.at[sem])
            copies[name, part].start()
            sem += 1

    for name in ("hidden", "in_gain", "q_gain", "k_gain"):
        copies[name, 0].wait()
    states = hidden[...].astype(F32)
    mean_sq = jnp.mean(states * states, axis=-1, keepdims=True)
    normed = (states * lax.rsqrt(mean_sq + 1e-06) * in_gain[...].astype(F32).reshape(1, width)).astype(BF16)

    depth = width // qkv_parts
    projected = None
    for part in range(qkv_parts):
        copies["qkv", part].wait()
        term = jnp.dot(
            normed[:, part * depth : (part + 1) * depth],
            qkv[part * depth : (part + 1) * depth, :],
            preferred_element_type=F32,
        )
        projected = term if projected is None else projected + term

    cosine = cos_ref[...]
    sine = sin_ref[...]

    def norm_rotate(block, gain):
        mean = jnp.mean(block * block, axis=-1, keepdims=True)
        block = block * lax.rsqrt(mean + 1e-06) * gain
        swapped = jnp.concatenate([block[:, HEAD // 2 :], block[:, : HEAD // 2]], axis=-1)
        return block * cosine + swapped * sine

    q_scale = q_gain[...].astype(F32).reshape(1, HEAD)
    k_scale = k_gain[...].astype(F32).reshape(1, HEAD)
    queries = jnp.concatenate(
        [norm_rotate(projected[:, j * HEAD : (j + 1) * HEAD], q_scale) for j in range(GROUP)], axis=0
    ).astype(BF16)
    blank = jnp.zeros((ROWS - STEPS, HEAD), F32)
    keys_new = jnp.concatenate(
        [norm_rotate(projected[:, GROUP * HEAD : (GROUP + 1) * HEAD], k_scale), blank],
        axis=0,
    ).astype(BF16)
    values_new = jnp.concatenate([projected[:, (GROUP + 1) * HEAD :], blank], axis=0).astype(BF16)

    length = length_ref[0]
    scale = 1.0 / jnp.sqrt(F32(HEAD))
    contract = (((1,), (1,)), ((), ()))
    new = lax.dot_general(queries, keys_new, contract, preferred_element_type=F32) * scale
    row = lax.broadcasted_iota(jnp.int32, (ROWS, ROWS), 0) % STEPS
    step_ok = lax.broadcasted_iota(jnp.int32, (ROWS, ROWS), 1) <= row
    new = jnp.where(step_ok, new, -1e30)
    top = jnp.max(new, axis=-1, keepdims=True)
    span = slots // key_parts
    for part in range(key_parts):
        copies["keys", part].wait()
        score = lax.dot_general(
            queries, keys[part * span : (part + 1) * span, :], contract, preferred_element_type=F32
        ) * scale
        slot = lax.broadcasted_iota(jnp.int32, (ROWS, span), 1) + part * span
        score = jnp.where(slot < length, score, -1e30)
        scores[:, part * span : (part + 1) * span] = score
        top = jnp.maximum(top, jnp.max(score, axis=-1, keepdims=True))
    exp_new = jnp.where(step_ok, jnp.exp(new - top), 0.0)
    total = jnp.sum(exp_new, axis=-1, keepdims=True)
    for part in range(key_parts):
        exp_old = jnp.exp(scores[:, part * span : (part + 1) * span] - top)
        scores[:, part * span : (part + 1) * span] = exp_old
        total = total + jnp.sum(exp_old, axis=-1, keepdims=True)
    weight_new = (exp_new / total).astype(BF16)
    mixed = jnp.dot(weight_new, values_new, preferred_element_type=F32)
    span = slots // value_parts
    for part in range(value_parts):
        copies["values", part].wait()
        weight = (scores[:, part * span : (part + 1) * span] / total).astype(BF16)
        mixed = mixed + jnp.dot(
            weight, values[part * span : (part + 1) * span, :], preferred_element_type=F32
        )
    heads = jnp.concatenate([mixed[j * STEPS : (j + 1) * STEPS, :] for j in range(GROUP)], axis=-1)
    heads = heads.astype(BF16)
    partial = None
    depth = wout.shape[0] // out_parts
    for part in range(out_parts):
        copies["out", part].wait()
        term = jnp.dot(
            heads[:, part * depth : (part + 1) * depth],
            wout[part * depth : (part + 1) * depth, :],
            preferred_element_type=F32,
        )
        partial = term if partial is None else partial + term
    partial_ref[...] = partial.astype(BF16)


def attention(hidden, in_gain, old_qkv, old_out, q_gain, k_gain, cache_keys, stored_values, cache_lengths):
    width = hidden.shape[-1]
    slots = cache_keys.shape[1]
    cosine, sine = rope_tables(cache_lengths)
    vmem = pl.BlockSpec(memory_space=pltpu.VMEM)
    hbm = pl.BlockSpec(memory_space=pltpu.HBM)
    return pl.pallas_call(
        attention_kernel,
        out_shape=jax.ShapeDtypeStruct((STEPS, width), BF16),
        in_specs=[pl.BlockSpec(memory_space=pltpu.SMEM)] + [vmem] * 2 + [hbm] * 8,
        out_specs=vmem,
        scratch_shapes=[
            pltpu.VMEM((STEPS, width), BF16),
            pltpu.VMEM(in_gain.shape, BF16),
            pltpu.VMEM(q_gain.shape, BF16),
            pltpu.VMEM(k_gain.shape, BF16),
            pltpu.VMEM(old_qkv.shape, BF16),
            pltpu.VMEM((slots, HEAD), BF16),
            pltpu.VMEM((slots, HEAD), BF16),
            pltpu.VMEM(old_out.shape, BF16),
            pltpu.VMEM((ROWS, slots), F32),
            pltpu.SemaphoreType.DMA((17,)),
        ],
        compiler_params=pltpu.CompilerParams(vmem_limit_bytes=60 * 1024 * 1024),
        cost_estimate=pl.CostEstimate(flops=120_000_000, bytes_accessed=17_400_000, transcendentals=140_000),
        name="attention",
    )(
        cache_lengths, cosine, sine, hidden.reshape(STEPS, width), in_gain, q_gain, k_gain, old_qkv,
        cache_keys.reshape(slots, HEAD),
        stored_values.reshape(slots, HEAD), old_out,
    )


def place(pieces, shape, previous=None):
    slots = jnp.stack([piece[3] for piece in pieces]).astype(jnp.int32)
    arrays = []
    for piece in pieces:
        if all(piece[0] is not array for array in arrays):
            arrays.append(piece[0])
    which = [next(i for i, array in enumerate(arrays) if array is piece[0]) for piece in pieces]
    count = len(arrays)

    def kernel(slots_ref, *refs):
        sources, out, sems = refs[:count], refs[-2], refs[-1]
        copies = []
        for i, (_, first, size, _, start) in enumerate(pieces):
            copy = pltpu.make_async_copy(
                sources[which[i]].at[pl.ds(first, size)],
                out.at[slots_ref[i], pl.ds(start, size)],
                sems.at[i],
            )
            copy.start()
            copies.append(copy)
        for copy in copies:
            copy.wait()

    operands = [slots] + arrays + ([] if previous is None else [previous])
    size = sum(array.size for array in arrays) * 2
    return pl.pallas_call(
        kernel,
        out_shape=jax.ShapeDtypeStruct(shape, BF16),
        in_specs=[pl.BlockSpec(memory_space=pltpu.SMEM)]
        + [pl.BlockSpec(memory_space=pltpu.VMEM)] * count
        + [pl.BlockSpec(memory_space=pl.ANY)] * (previous is not None),
        out_specs=pl.BlockSpec(memory_space=pl.ANY),
        scratch_shapes=[pltpu.SemaphoreType.DMA((len(pieces),))],
        compiler_params=pltpu.CompilerParams(vmem_limit_bytes=16 * 1024 * 1024),
        input_output_aliases={} if previous is None else {len(operands) - 1: 0},
        cost_estimate=pl.CostEstimate(flops=0, bytes_accessed=2 * size, transcendentals=0),
        name="place",
    )(*operands)


def swap(array, axis):
    return lax.ppermute(array, axis, [(0, 1), (1, 0)])


def ring(array):
    pairs = []
    for x in range(4):
        pairs += [(2 * x, (x + 1) % 4 * 2), (2 * x + 1, (x + 3) % 4 * 2 + 1)]
    return lax.ppermute(array, ("x", "core"), pairs)


def body(
    hidden, in_gain, old_qkv, old_out, q_gain, k_gain, cache_keys, stored_values, cache_lengths, new_qkv
):
    rows, columns = new_qkv.shape
    tp = lax.axis_size(TP)
    rep = lax.axis_size(REP)
    z, x, core = lax.axis_index("z_hi"), lax.axis_index("x"), lax.axis_index("core")
    back = 2 * core + 3

    def slot(dz, dx, dc):
        return ((z + dz) % 2 * 4 + (x + dx) % 4) * 2 + (core + dc) % 2

    blocks = new_qkv.reshape(rows, tp, columns // tp).transpose(1, 0, 2)
    own = lax.all_to_all(blocks, TP, split_axis=0, concat_axis=0, tiled=True)
    partial = attention(
        hidden, in_gain, old_qkv, old_out, q_gain, k_gain, cache_keys, stored_values, cache_lengths
    )
    own, partial = lax.optimization_barrier((own, partial))
    shape = (rep, tp, rows, columns // tp)

    other = swap(own, "z_hi")
    core_own = swap(own, "core")
    near = ring(own)
    near_pair = ring(core_own)
    near_pair, partial = lax.optimization_barrier((near_pair, partial))
    pair = swap(partial, "z_lo")
    partial = (partial.astype(F32) + pair.astype(F32)).astype(BF16)
    partial = jnp.broadcast_to(partial[None], (4,) + partial.shape)
    out = place(
        [
            (own, 0, tp, slot(0, 0, 0), 0),
            (core_own, 0, tp, slot(0, 0, 1), 0),
            (near, 0, tp, slot(0, back, 0), 0),
        ],
        shape,
    )
    far = ring(near)
    core_near = swap(near, "core")
    core_near_pair = swap(near_pair, "core")
    core_far = swap(far, "core")
    other_far = swap(far, "z_hi")
    other, out = lax.optimization_barrier((other, out))
    other_near = ring(other)
    core_other = swap(other, "core")
    core_other, partial = lax.optimization_barrier((core_other, partial))
    terms = lax.all_to_all(partial, "y", split_axis=0, concat_axis=0, tiled=True)
    other_near_pair = ring(core_other)
    out = place(
        [
            (near_pair, 0, tp, slot(0, back, 1), 0),
            (core_near, 0, tp, slot(0, -back, 1), 0),
            (core_near_pair, 0, tp, slot(0, -back, 0), 0),
            (other, 0, tp, slot(1, 0, 0), 0),
            (core_other, 0, tp, slot(1, 0, 1), 0),
            (far, 0, tp, slot(0, 2, 0), 0),
            (core_far, 0, tp, slot(0, 2, 1), 0),
        ],
        shape,
        out,
    )
    other_near, other_near_pair, other_far, out = lax.optimization_barrier((other_near, other_near_pair, other_far, out))
    core_other_near = swap(other_near, "core")
    core_other_near_pair = swap(other_near_pair, "core")
    core_other_far = swap(other_far, "core")
    attended = terms[0].astype(F32)
    for peer in range(1, 4):
        attended = attended + terms[peer].astype(F32)
    attended = attended.astype(BF16)
    out = place(
        [
            (other_near, 0, tp, slot(1, back, 0), 0),
            (core_other_near, 0, tp, slot(1, -back, 1), 0),
            (other_near_pair, 0, tp, slot(1, back, 1), 0),
            (core_other_near_pair, 0, tp, slot(1, -back, 0), 0),
            (other_far, 0, tp, slot(1, 2, 0), 0),
            (core_other_far, 0, tp, slot(1, 2, 1), 0),
        ],
        shape,
        out,
    )
    return attended.reshape(hidden.shape), out.reshape(rep * tp * rows, columns // tp)


def solution(mesh):
    fine = jax.sharding.Mesh(mesh.devices.reshape(2, 4, 2, 4, 2), REP + TP)
    in_specs = (
        P(REP, None, None),
        P(),
        P(None, TP),
        P(TP, None),
        P(),
        P(),
        P(REP, None, TP, None),
        P(REP, None, TP, None),
        P(REP),
        P(REP + TP, None),
    )
    out_specs = (P(REP, None, None), P(None, TP))
    return jax.shard_map(body, mesh=fine, in_specs=in_specs, out_specs=out_specs, check_vma=False)
```
